32 devices in a mesh: ty: 8 (over z, y), tx: 4 (over x, core).
Axes of the slice: x: 2, y: 2, z: 4, core: 2. Of those that a mesh axis runs over, the one named last changes fastest.
Arguments:
- object_tiles: float32 [2, 2, 2048, 1024], P(None, None, 'ty', 'tx'), may hold values from -5 to 5
- probe_field: float32 [2, 256, 256], replicated, may hold values from -6 to 6
- prop_angle: float32 [256, 256], replicated, may hold values from -3.140625 to 3.140625
- scan_offsets: int32 [2, 8, 4, 2, 2], P(None, 'ty', 'tx'), may hold values from 0 to 255, as said below
- probe_counts: int32 [2, 8, 4], P(None, 'ty', 'tx'), may hold values from 0 to 2, as said below
- amplitudes: float32 [2, 8, 4, 2, 256, 256], P(None, 'ty', 'tx'), may hold values from 0 to 2.5
Outputs:
- object_out: float32 [2, 2, 2048, 1024], P(None, None, 'ty', 'tx')
The draws below stay inside these ranges and needn't reach their ends.
Inputs may be any that keep to these rules, and one draw needn't show every extreme that they name: `probe_counts`: every tile has at most 2 live slots in an iteration, and some tile has exactly 2 in every iteration; slots at or past a tile's count are not used. `scan_offsets`: on tiles of the last tile row the row offset is at most 0, and on tiles of the last tile column the column offset is at most 0, so every window lies inside the object.
All inputs are finite; a program needn't handle non-finite values.
Results may differ from the reference program's by a relative error of at most 0.0003.
Values sent between devices are 32-bit elements; how exact they have to be, the bound alone decides.
A program may use at most 128 MiB of HBM per device.

```python
import jax
import jax.numpy as jnp
from jax import lax

PROBE = 256
TILE = 256
P_MAX = 2
ITERS = 2
TILE_ROWS = 8
TILE_COLS = 4
NY = 2048
NX = 1024


def draw_scan_offsets(key, part):
    array_shape = (ITERS, TILE_ROWS, TILE_COLS, P_MAX, 2)
    raw_bits = jax.random.randint(key, array_shape, 0, 1 << 20)
    iter_ids = lax.broadcasted_iota(jnp.int32, array_shape, 0)
    row_ids = lax.broadcasted_iota(jnp.int32, array_shape, 1)
    col_ids = lax.broadcasted_iota(jnp.int32, array_shape, 2)
    slot_ids = lax.broadcasted_iota(jnp.int32, array_shape, 3)
    coord_ids = lax.broadcasted_iota(jnp.int32, array_shape, 4)
    last_edge = jnp.where(coord_ids == 0, row_ids == TILE_ROWS - 1, col_ids == TILE_COLS - 1)
    upper_bound = jnp.where(last_edge, TILE - PROBE + 1, TILE)
    values = raw_bits % upper_bound
    picked_idx = jax.random.randint(jax.random.fold_in(key, 7), (4,), 0, 1 << 20)
    far_row = picked_idx[0] % (TILE_ROWS - 1)
    far_col = picked_idx[1] % (TILE_COLS - 1)
    near_row = picked_idx[2] % TILE_ROWS
    near_col = picked_idx[3] % TILE_COLS
    far_spot = (iter_ids == 0) & (row_ids == far_row) & (col_ids == far_col) & (slot_ids == 0)
    values = jnp.where(far_spot, TILE - 1, values)
    near_spot = (iter_ids == 0) & (row_ids == near_row) & (col_ids == near_col) & (slot_ids == P_MAX - 1)
    values = jnp.where(near_spot, 0, values)
    return values.astype(jnp.int32)


def draw_probe_counts(key, part):
    array_shape = (ITERS, TILE_ROWS, TILE_COLS)
    base_counts = jax.random.randint(key, array_shape, 0, P_MAX + 1)
    busiest = jax.random.randint(jax.random.fold_in(key, 11), (ITERS, 1, 1), 0, TILE_ROWS * TILE_COLS)
    flat_ids = lax.broadcasted_iota(jnp.int32, array_shape, 1) * TILE_COLS + lax.broadcasted_iota(jnp.int32, array_shape, 2)
    return jnp.where(flat_ids == busiest, P_MAX, base_counts).astype(jnp.int32)


def steps_of(stream_key, extent, split, smallest, largest):
    level = 1.0
    for dim, parts in split:
        heights = jax.random.uniform(jax.random.fold_in(jax.random.fold_in(stream_key, 6), dim), (parts,), jnp.float32, smallest / len(split), largest / len(split))
        level = level * jnp.repeat(jnp.exp(heights), extent[dim] // parts).reshape((-1,) + (1,) * (len(extent) - 1 - dim))
    return level


def normal_values(stream_key, extent, deviation, bound, shards=(), held_as=jnp.bfloat16):
    level = steps_of(stream_key, extent, shards, -0.22, 0.18) if shards else 1.0
    drawn = jax.random.normal(stream_key, extent, jnp.float32) * deviation * level
    return jnp.minimum(jnp.maximum(drawn, -bound), bound).astype(held_as)


def setup_inputs(seed: int = 0) -> dict:
    key_list = jax.random.split(jax.random.key(seed), 7)
    object_tiles = normal_values(key_list[0], (2, 2, NY, NX), 0.7, 5.0, ((2, 8), (3, 4)), jnp.float32)
    probe_field = normal_values(key_list[1], (2, PROBE, PROBE), 1.0, 6.0, (), jnp.float32)
    prop_angle = jnp.clip(jax.random.uniform(key_list[2], (PROBE, PROBE), jnp.float32, -3.140625, 3.140625), -3.140625, 3.140625)
    scan_offsets = draw_scan_offsets(jax.random.fold_in(key_list[6], 71), 0)
    probe_counts = draw_probe_counts(jax.random.fold_in(key_list[6], 71), 0)
    amplitudes = jnp.clip(2.5 * jax.random.uniform(key_list[5], (ITERS, TILE_ROWS, TILE_COLS, P_MAX, PROBE, PROBE), jnp.float32) ** steps_of(key_list[5], (ITERS, TILE_ROWS, TILE_COLS, P_MAX, PROBE, PROBE), ((1, 8), (2, 4)), -0.2, 0.2), 0.0, 2.5)
    return {"object_tiles": object_tiles, "probe_field": probe_field, "prop_angle": prop_angle, "scan_offsets": scan_offsets, "probe_counts": probe_counts, "amplitudes": amplitudes}


soft_floor = 0.01
step_size = 0.25

def spectrum(real_part, imag_part, inverse):
    field = lax.complex(real_part, imag_part)
    if inverse:
        result = jnp.fft.ifft2(field, norm='ortho')
    else:
        result = jnp.fft.fft2(field, norm='ortho')
    return (jnp.real(result), jnp.imag(result))

def window_gradient(window, probe_field, kernel_re, kernel_im, measured_amp, transform):
    one_re, one_im = (window[0, 0], window[0, 1])
    two_re, two_im = (window[1, 0], window[1, 1])
    probe_re, probe_im = (probe_field[0], probe_field[1])
    first_re = probe_re * one_re - probe_im * one_im
    first_im = probe_re * one_im + probe_im * one_re
    freq_re, freq_im = transform(first_re, first_im, False)
    moved_re = freq_re * kernel_re - freq_im * kernel_im
    moved_im = freq_re * kernel_im + freq_im * kernel_re
    mid_re, mid_im = transform(moved_re, moved_im, True)
    second_re = mid_re * two_re - mid_im * two_im
    second_im = mid_re * two_im + mid_im * two_re
    far_re, far_im = transform(second_re, second_im, False)
    magnitude = jnp.sqrt(far_re * far_re + far_im * far_im + soft_floor)
    factor = 1.0 - measured_amp / magnitude
    back_re, back_im = transform(far_re * factor, far_im * factor, True)
    grad_two_re = mid_re * back_re + mid_im * back_im
    grad_two_im = mid_re * back_im - mid_im * back_re
    carry_re = two_re * back_re + two_im * back_im
    carry_im = two_re * back_im - two_im * back_re
    spec_re, spec_im = transform(carry_re, carry_im, False)
    turned_re = spec_re * kernel_re + spec_im * kernel_im
    turned_im = spec_im * kernel_re - spec_re * kernel_im
    early_re, early_im = transform(turned_re, turned_im, True)
    grad_one_re = probe_re * early_re + probe_im * early_im
    grad_one_im = probe_re * early_im - probe_im * early_re
    return jnp.stack([jnp.stack([grad_one_re, grad_one_im]), jnp.stack([grad_two_re, grad_two_im])])

def reference(object_tiles, probe_field, prop_angle, scan_offsets, probe_counts, amplitudes):
    kernel_re = jnp.cos(prop_angle)
    kernel_im = jnp.sin(prop_angle)
    slot_total = TILE_ROWS * TILE_COLS * P_MAX
    slot_ids = lax.iota(jnp.int32, slot_total)
    tile_ids = slot_ids // P_MAX
    row_ids = tile_ids // TILE_COLS
    col_ids = tile_ids % TILE_COLS
    slot_in_tile = slot_ids % P_MAX
    zero_index = jnp.zeros((), jnp.int32)
    current = object_tiles
    for iteration in range(ITERS):
        offsets = scan_offsets[iteration].reshape(slot_total, 2)
        counts_here = probe_counts[iteration].reshape(TILE_ROWS * TILE_COLS)
        live_mask = (slot_in_tile < counts_here[tile_ids]).astype(jnp.float32)
        corner_rows = (row_ids * TILE + offsets[:, 0]).astype(jnp.int32)
        corner_cols = (col_ids * TILE + offsets[:, 1]).astype(jnp.int32)
        measured = amplitudes[iteration].reshape(slot_total, PROBE, PROBE)

        def accumulate(running, inputs, frozen=current):
            corner_row, corner_col, weight, measured_amp = inputs
            start_index = (zero_index, zero_index, corner_row.astype(jnp.int32), corner_col.astype(jnp.int32))
            window = lax.dynamic_slice(frozen, start_index, (2, 2, PROBE, PROBE))
            contrib = window_gradient(window, probe_field, kernel_re, kernel_im, measured_amp, spectrum) * weight
            placed = lax.dynamic_slice(running, start_index, (2, 2, PROBE, PROBE)) + contrib
            return (lax.dynamic_update_slice(running, placed, start_index), None)
        gradient, unused = lax.scan(accumulate, jnp.zeros_like(current), (corner_rows, corner_cols, live_mask, measured))
        current = current - step_size * gradient
    return current
```

```python
import functools
import math

import jax
import jax.numpy as jnp
import ml_dtypes
import numpy as np
from jax import lax
from jax.experimental import pallas as pl
from jax.experimental.pallas import tpu as pltpu
from jax.sharding import PartitionSpec as P

MESH = pl.DeviceIdType.MESH
SOFT_FLOOR = 0.01
STEP_SIZE = 0.25
ROWS = 32
OWN, RIGHT, BELOW, DIAG = range(4)
UP, LEFT, FWD, GOWN, GBELOW, GDOWN = range(6)


def dft_tables(n):
    index = np.arange(n)
    angles = (index[:, None] * index[None, :] % n) * (2.0 * math.pi / n)
    re, im = np.cos(angles) / math.sqrt(n), -np.sin(angles) / math.sqrt(n)

    def terms(table):
        hi = table.astype(np.float32).astype(ml_dtypes.bfloat16)
        return hi, (table - hi.astype(np.float64)).astype(np.float32).astype(ml_dtypes.bfloat16)

    left_hi, left_lo = terms(np.block([[re, -im], [im, re]]))
    right_hi, right_lo = terms(np.block([[re, im], [-im, re]]))
    return (
        np.concatenate([left_hi, left_hi, left_lo], axis=1),
        np.concatenate([right_hi, right_hi, right_lo], axis=0),
    )


def roll_kernel(offsets, probe, rolled):
    iters, slots = rolled.shape[:2]
    for it in range(iters):
        for s in range(slots):
            for part in range(2):
                value = pltpu.roll(probe[part], offsets[it, 0, 0, s, 0], 0)
                rolled[it, s, part] = pltpu.roll(value, offsets[it, 0, 0, s, 1], 1)


def kernel(
    ny, nx, offsets, counts, obj, rolled, prop, amps, left_table, right_table, out,
    cur, halo, grads, got, a_buf, z_buf, b_buf, y_buf, mid_buf, win_buf, send_sem, recv_sem,
):
    n = obj.shape[2]
    iters, slots = rolled.shape[:2]
    ty, tx = lax.axis_index("ty"), lax.axis_index("tx")
    up, down = (lax.rem(ty + ny - 1, ny), tx), (lax.rem(ty + 1, ny), tx)
    left, right = (ty, lax.rem(tx + nx - 1, nx)), (ty, lax.rem(tx + 1, nx))

    barrier = pltpu.get_barrier_semaphore()
    for neighbour in (up, down, left, right):
        pl.semaphore_signal(barrier, inc=1, device_id=neighbour, device_id_type=MESH)
    pl.semaphore_wait(barrier, 4)

    def tile(it, k):
        return obj.at[k // 2, k % 2] if it == 0 else cur.at[k // 2, k % 2]

    def copy(it, kind, k):
        src, dst, target = {
            UP: lambda: (tile(it, k), halo.at[it, BELOW, k], up),
            LEFT: lambda: (tile(it, k), halo.at[it, RIGHT, k], left),
            FWD: lambda: (halo.at[it, BELOW, k], halo.at[it, DIAG, k], left),
            GOWN: lambda: (grads.at[it, RIGHT, k], got.at[it, 0, k], right),
            GBELOW: lambda: (grads.at[it, DIAG, k], got.at[it, 1, k], right),
            GDOWN: lambda: (grads.at[it, BELOW, k], got.at[it, 2, k], down),
        }[kind]()
        return pltpu.make_async_remote_copy(
            src_ref=src, dst_ref=dst, send_sem=send_sem.at[it, kind, k], recv_sem=recv_sem.at[it, kind, k],
            device_id=target, device_id_type=MESH,
        )

    def by_rows(body):
        def step(i, carry):
            body(pl.multiple_of(i * ROWS, ROWS))
            return carry

        lax.fori_loop(0, n // ROWS, step, 0, unroll=2)

    def split(value):
        hi = value.astype(jnp.bfloat16)
        return hi, (value - hi.astype(jnp.float32)).astype(jnp.bfloat16)

    def put(s, row, re, im):
        for part, value in enumerate((re, im)):
            hi, lo = split(value)
            for block, term in ((part, hi), (part + 2, lo), (part + 4, hi)):
                a_buf[pl.ds(block * n + row, ROWS), s * n:(s + 1) * n] = term

    def transform():
        z_buf[...] = jnp.dot(left_table[...], a_buf[...], preferred_element_type=jnp.float32)

        def middle(row):
            for s in range(slots):
                for part in range(2):
                    hi, lo = split(z_buf[pl.ds(part * n + row, ROWS), s * n:(s + 1) * n])
                    for block, term in ((part, hi), (part + 2, lo), (part + 4, hi)):
                        b_buf[pl.ds(s * n + row, ROWS), block * n:(block + 1) * n] = term

        by_rows(middle)
        y_buf[...] = jnp.dot(b_buf[...], right_table[...], preferred_element_type=jnp.float32)

    def result(s, row):
        rows = pl.ds(s * n + row, ROWS)
        return y_buf[rows, :n], y_buf[rows, n:]

    def masks(it, s, row):
        shape = (ROWS, n)
        under = lax.broadcasted_iota(jnp.int32, shape, 0) + row < offsets[it, 0, 0, s, 0]
        beside = lax.broadcasted_iota(jnp.int32, shape, 1) < offsets[it, 0, 0, s, 1]
        return under, beside

    def window(it, s, row, k):
        under, beside = masks(it, s, row)
        rows = pl.ds(row, ROWS)
        inner = jnp.where(beside, halo[it, RIGHT, k, rows, :], tile(it, k)[rows, :])
        outer = jnp.where(beside, halo[it, DIAG, k, rows, :], halo[it, BELOW, k, rows, :])
        return jnp.where(under, outer, inner)

    def place(it, row, k, values):
        rows = pl.ds(row, ROWS)
        sums = [0.0] * 4
        for s, value in enumerate(values):
            under, beside = masks(it, s, row)
            value = value * (s < counts[it, 0, 0]).astype(jnp.float32)
            high, low = jnp.where(under, 0.0, value), jnp.where(under, value, 0.0)
            sums[OWN] += jnp.where(beside, 0.0, high)
            sums[RIGHT] += jnp.where(beside, high, 0.0)
            sums[BELOW] += jnp.where(beside, 0.0, low)
            sums[DIAG] += jnp.where(beside, low, 0.0)
        for quarter in range(4):
            grads[it, quarter, k, rows, :] = sums[quarter]

    def give_right(it, layer):
        for kind in (GBELOW, GOWN):
            for k in (2 * layer, 2 * layer + 1):
                copy(it, kind, k).start()

    def give_down(it, layer):
        for k in (2 * layer, 2 * layer + 1):
            copy(it, GBELOW, k).wait_recv()

            def add(row):
                rows = pl.ds(row, ROWS)
                grads[it, BELOW, k, rows, :] += got[it, 1, k, rows, :]

            by_rows(add)
            copy(it, GDOWN, k).start()

    def update(it, layer):
        last = it == iters - 1
        for k in (2 * layer, 2 * layer + 1):
            copy(it, GOWN, k).wait_recv()
            copy(it, GDOWN, k).wait_recv()

            def step(row):
                rows = pl.ds(row, ROWS)
                total = grads[it, OWN, k, rows, :] + got[it, 0, k, rows, :] + got[it, 2, k, rows, :]
                target = out if last else cur
                target[k // 2, k % 2, rows, :] = tile(it, k)[rows, :] - STEP_SIZE * total

            by_rows(step)
            if not last:
                copy(it + 1, UP, k).start()
                copy(it + 1, LEFT, k).start()

    for k in range(4):
        copy(0, UP, k).start()
        copy(0, LEFT, k).start()

    for it in range(iters):
        for k in ((0, 1, 2, 3) if it == 0 else (2, 3, 0, 1)):
            copy(it, UP, k).wait_recv()
            copy(it, FWD, k).start()
        for k in (0, 1):
            copy(it, LEFT, k).wait_recv()
            copy(it, FWD, k).wait_recv()

        def first(row):
            rows = pl.ds(row, ROWS)
            for s in range(slots):
                re, im = window(it, s, row, 0), window(it, s, row, 1)
                p_re, p_im = rolled[it, s, 0, rows, :], rolled[it, s, 1, rows, :]
                put(s, row, p_re * re - p_im * im, p_re * im + p_im * re)

        by_rows(first)
        transform()

        def propagate(row):
            rows = pl.ds(row, ROWS)
            h_re, h_im = prop[0, rows, :], prop[1, rows, :]
            for s in range(slots):
                re, im = result(s, row)
                put(s, row, re * h_im + im * h_re, re * h_re - im * h_im)

        by_rows(propagate)
        transform()
        for k in (2, 3):
            copy(it, LEFT, k).wait_recv()
            copy(it, FWD, k).wait_recv()

        def second(row):
            rows = pl.ds(row, ROWS)
            for s in range(slots):
                m_im, m_re = result(s, row)
                re, im = window(it, s, row, 2), window(it, s, row, 3)
                mid_buf[s, 0, rows, :], mid_buf[s, 1, rows, :] = m_re, m_im
                win_buf[s, 0, rows, :], win_buf[s, 1, rows, :] = re, im
                put(s, row, m_re * re - m_im * im, m_re * im + m_im * re)

        by_rows(second)
        transform()

        def compare(row):
            rows = pl.ds(row, ROWS)
            for s in range(slots):
                re, im = result(s, row)
                factor = 1.0 - amps[it, 0, 0, s, rows, :] * lax.rsqrt(re * re + im * im + SOFT_FLOOR)
                put(s, row, im * factor, re * factor)

        by_rows(compare)
        transform()

        def back(row):
            rows = pl.ds(row, ROWS)
            found = [[], []]
            for s in range(slots):
                im, re = result(s, row)
                m_re, m_im = mid_buf[s, 0, rows, :], mid_buf[s, 1, rows, :]
                w_re, w_im = win_buf[s, 0, rows, :], win_buf[s, 1, rows, :]
                found[0].append(m_re * re + m_im * im)
                found[1].append(m_re * im - m_im * re)
                put(s, row, w_re * re + w_im * im, w_re * im - w_im * re)
            place(it, row, 2, found[0])
            place(it, row, 3, found[1])

        by_rows(back)
        give_right(it, 1)
        transform()

        def turn(row):
            rows = pl.ds(row, ROWS)
            h_re, h_im = prop[0, rows, :], prop[1, rows, :]
            for s in range(slots):
                re, im = result(s, row)
                put(s, row, im * h_re - re * h_im, re * h_re + im * h_im)

        by_rows(turn)
        transform()

        def early(row):
            rows = pl.ds(row, ROWS)
            found = [[], []]
            for s in range(slots):
                im, re = result(s, row)
                p_re, p_im = rolled[it, s, 0, rows, :], rolled[it, s, 1, rows, :]
                found[0].append(p_re * re + p_im * im)
                found[1].append(p_re * im - p_im * re)
            place(it, row, 0, found[0])
            place(it, row, 1, found[1])

        by_rows(early)
        give_right(it, 0)
        give_down(it, 1)
        give_down(it, 0)
        update(it, 1)
        update(it, 0)

    for it in range(iters):
        for kind in range(6):
            for k in range(4):
                copy(it, kind, k).wait_send()


def shards(ny, nx, object_tiles, probe_field, prop_angle, scan_offsets, probe_counts, amplitudes):
    n = object_tiles.shape[2]
    iters, slots = scan_offsets.shape[0], scan_offsets.shape[3]
    left_table, right_table = dft_tables(n)
    vmem, smem = pl.BlockSpec(memory_space=pltpu.VMEM), pl.BlockSpec(memory_space=pltpu.SMEM)
    rolled = pl.pallas_call(
        roll_kernel,
        out_shape=jax.ShapeDtypeStruct((iters, slots, 2, n, n), jnp.float32),
        in_specs=[smem, vmem],
        out_specs=vmem,
        compiler_params=pltpu.CompilerParams(vmem_limit_bytes=32 * 2**20),
    )(scan_offsets, probe_field)
    prop = jnp.stack([jnp.cos(prop_angle), jnp.sin(prop_angle)])
    f32, bf16 = jnp.float32, jnp.bfloat16
    return pl.pallas_call(
        functools.partial(kernel, ny, nx),
        out_shape=jax.ShapeDtypeStruct(object_tiles.shape, f32),
        in_specs=[smem, smem] + [vmem] * 6,
        out_specs=vmem,
        scratch_shapes=[
            pltpu.VMEM(object_tiles.shape, f32),
            pltpu.VMEM((iters, 4, 4, n, n), f32),
            pltpu.VMEM((iters, 4, 4, n, n), f32),
            pltpu.VMEM((iters, 3, 4, n, n), f32),
            pltpu.VMEM((6 * n, slots * n), bf16),
            pltpu.VMEM((2 * n, slots * n), f32),
            pltpu.VMEM((slots * n, 6 * n), bf16),
            pltpu.VMEM((slots * n, 2 * n), f32),
            pltpu.VMEM((slots, 2, n, n), f32),
            pltpu.VMEM((slots, 2, n, n), f32),
            pltpu.SemaphoreType.DMA((iters, 6, 4)),
            pltpu.SemaphoreType.DMA((iters, 6, 4)),
        ],
        compiler_params=pltpu.CompilerParams(
            collective_id=0, has_side_effects=True, vmem_limit_bytes=56 * 2**20
        ),
    )(scan_offsets, probe_counts, object_tiles, rolled, prop, amplitudes,
      jnp.asarray(left_table), jnp.asarray(right_table))


def solution(mesh):
    in_specs = (
        P(None, None, "ty", "tx"),
        P(),
        P(),
        P(None, "ty", "tx", None, None),
        P(None, "ty", "tx"),
        P(None, "ty", "tx", None, None, None),
    )
    return jax.shard_map(
        functools.partial(shards, mesh.shape["ty"], mesh.shape["tx"]),
        mesh=mesh, in_specs=in_specs, out_specs=P(None, None, "ty", "tx"), check_vma=False,
    )
```

```python
import functools
import math

import jax
import jax.numpy as jnp
import ml_dtypes
import numpy as np
from jax import lax
from jax.experimental import pallas as pl
from jax.experimental.pallas import tpu as pltpu
from jax.sharding import PartitionSpec as P

MESH = pl.DeviceIdType.MESH
SOFT_FLOOR = 0.01
STEP_SIZE = 0.25
ROWS = 32
OWN, RIGHT, BELOW, DIAG = range(4)
UP, LEFT, FWD, GOWN, GBELOW, GDOWN = range(6)


def dft_tables(n):
    index = np.arange(n)
    angles = (index[:, None] * index[None, :] % n) * (2.0 * math.pi / n)
    re, im = np.cos(angles) / math.sqrt(n), -np.sin(angles) / math.sqrt(n)

    def terms(table):
        hi = table.astype(np.float32).astype(ml_dtypes.bfloat16)
        return hi, (table - hi.astype(np.float64)).astype(np.float32).astype(ml_dtypes.bfloat16)

    left_hi, left_lo = terms(np.block([[re, -im], [im, re]]))
    right_hi, right_lo = terms(np.block([[re, im], [-im, re]]))
    return (
        np.concatenate([left_hi, left_hi, left_lo], axis=1),
        np.concatenate([right_hi, right_hi, right_lo], axis=0),
    )


def prepare_kernel(offsets, probe, angle, rolled, prop):
    prop[0], prop[1] = jnp.cos(angle[...]), jnp.sin(angle[...])
    iters, slots = rolled.shape[:2]
    for it in range(iters):
        for s in range(slots):
            for part in range(2):
                value = pltpu.roll(probe[part], offsets[it, 0, 0, s, 0], 0)
                rolled[it, s, part] = pltpu.roll(value, offsets[it, 0, 0, s, 1], 1)


def kernel(
    ny, nx, offsets, counts, obj_hbm, rolled_hbm, prop_hbm, amps_hbm, left_hbm, right_hbm, out,
    obj, rolled, prop, amps, left_table, right_table, load_sem, cur, halo, grads, got, a_buf, z_buf, b_buf, y_buf, mid_buf, win_buf, send_sem, recv_sem,
):
    n = obj.shape[2]
    iters, slots = rolled.shape[:2]
    loads = [
        pltpu.make_async_copy(source, target, load_sem.at[i])
        for i, (source, target) in enumerate((
            (obj_hbm, obj), (rolled_hbm, rolled), (left_hbm, left_table), (right_hbm, right_table),
            (prop_hbm, prop), (amps_hbm, amps),
        ))
    ]
    for load in loads:
        load.start()
    ty, tx = lax.axis_index("ty"), lax.axis_index("tx")
    up, down = (lax.rem(ty + ny - 1, ny), tx), (lax.rem(ty + 1, ny), tx)
    left, right = (ty, lax.rem(tx + nx - 1, nx)), (ty, lax.rem(tx + 1, nx))

    barrier = pltpu.get_barrier_semaphore()
    for neighbour in (up, down, left, right):
        pl.semaphore_signal(barrier, inc=1, device_id=neighbour, device_id_type=MESH)
    pl.semaphore_wait(barrier, 4)

    def tile(it, k):
        return obj.at[k // 2, k % 2] if it == 0 else cur.at[k // 2, k % 2]

    def copy(it, kind, k):
        source = obj_hbm.at[k // 2, k % 2] if it == 0 else tile(it, k)
        src, dst, target = {
            UP: lambda: (source, halo.at[it, BELOW, k], up),
            LEFT: lambda: (source, halo.at[it, RIGHT, k], left),
            FWD: lambda: (halo.at[it, BELOW, k], halo.at[it, DIAG, k], left),
            GOWN: lambda: (grads.at[it, RIGHT, k], got.at[it, 0, k], right),
            GBELOW: lambda: (grads.at[it, DIAG, k], got.at[it, 1, k], right),
            GDOWN: lambda: (grads.at[it, BELOW, k], got.at[it, 2, k], down),
        }[kind]()
        return pltpu.make_async_remote_copy(
            src_ref=src, dst_ref=dst, send_sem=send_sem.at[it, kind, k], recv_sem=recv_sem.at[it, kind, k],
            device_id=target, device_id_type=MESH,
        )

    def by_rows(body):
        def step(i, carry):
            body(pl.multiple_of(i * ROWS, ROWS))
            return carry

        lax.fori_loop(0, n // ROWS, step, 0, unroll=2)

    def split(value):
        hi = value.astype(jnp.bfloat16)
        return hi, (value - hi.astype(jnp.float32)).astype(jnp.bfloat16)

    def put(s, row, re, im):
        for part, value in enumerate((re, im)):
            hi, lo = split(value)
            for block, term in ((part, hi), (part + 2, lo), (part + 4, hi)):
                a_buf[pl.ds(block * n + row, ROWS), s * n:(s + 1) * n] = term

    def transform():
        z_buf[...] = jnp.dot(left_table[...], a_buf[...], preferred_element_type=jnp.float32)

        def middle(row):
            for s in range(slots):
                for part in range(2):
                    hi, lo = split(z_buf[pl.ds(part * n + row, ROWS), s * n:(s + 1) * n])
                    for block, term in ((part, hi), (part + 2, lo), (part + 4, hi)):
                        b_buf[pl.ds(s * n + row, ROWS), block * n:(block + 1) * n] = term

        by_rows(middle)
        y_buf[...] = jnp.dot(b_buf[...], right_table[...], preferred_element_type=jnp.float32)

    def result(s, row):
        rows = pl.ds(s * n + row, ROWS)
        return y_buf[rows, :n], y_buf[rows, n:]

    def masks(it, s, row):
        shape = (ROWS, n)
        under = lax.broadcasted_iota(jnp.int32, shape, 0) + row < offsets[it, 0, 0, s, 0]
        beside = lax.broadcasted_iota(jnp.int32, shape, 1) < offsets[it, 0, 0, s, 1]
        return under, beside

    def window(it, s, row, k):
        under, beside = masks(it, s, row)
        rows = pl.ds(row, ROWS)
        inner = jnp.where(beside, halo[it, RIGHT, k, rows, :], tile(it, k)[rows, :])
        outer = jnp.where(beside, halo[it, DIAG, k, rows, :], halo[it, BELOW, k, rows, :])
        return jnp.where(under, outer, inner)

    def place(it, row, k, values):
        rows = pl.ds(row, ROWS)
        sums = [0.0] * 4
        for s, value in enumerate(values):
            under, beside = masks(it, s, row)
            value = value * (s < counts[it, 0, 0]).astype(jnp.float32)
            high, low = jnp.where(under, 0.0, value), jnp.where(under, value, 0.0)
            sums[OWN] += jnp.where(beside, 0.0, high)
            sums[RIGHT] += jnp.where(beside, high, 0.0)
            sums[BELOW] += jnp.where(beside, 0.0, low)
            sums[DIAG] += jnp.where(beside, low, 0.0)
        for quarter in range(4):
            grads[it, quarter, k, rows, :] = sums[quarter]

    def give_right(it, layer):
        for kind in (GBELOW, GOWN):
            for k in (2 * layer, 2 * layer + 1):
                copy(it, kind, k).start()

    def give_down(it, layer):
        for k in (2 * layer, 2 * layer + 1):
            copy(it, GBELOW, k).wait_recv()

            def add(row):
                rows = pl.ds(row, ROWS)
                grads[it, BELOW, k, rows, :] += got[it, 1, k, rows, :]

            by_rows(add)
            copy(it, GDOWN, k).start()

    def update(it, k):
        copy(it, GOWN, k).wait_recv()
        copy(it, GDOWN, k).wait_recv()
        target = out if it == iters - 1 else cur

        def step(row):
            rows = pl.ds(row, ROWS)
            total = grads[it, OWN, k, rows, :] + got[it, 0, k, rows, :] + got[it, 2, k, rows, :]
            target[k // 2, k % 2, rows, :] = tile(it, k)[rows, :] - STEP_SIZE * total

        by_rows(step)

    def send(it, k):
        copy(it, UP, k).start()
        copy(it, LEFT, k).start()

    def forward(it, k):
        copy(it, UP, k).wait_recv()
        copy(it, FWD, k).start()

    def landed(it, k):
        copy(it, LEFT, k).wait_recv()
        copy(it, FWD, k).wait_recv()

    for k in range(4):
        send(0, k)
    for load in loads:
        load.wait()

    for it in range(iters):
        for k in (0, 1):
            forward(it, k)
        for k in (0, 1):
            landed(it, k)

        def first(row):
            rows = pl.ds(row, ROWS)
            for s in range(slots):
                re, im = window(it, s, row, 0), window(it, s, row, 1)
                p_re, p_im = rolled[it, s, 0, rows, :], rolled[it, s, 1, rows, :]
                put(s, row, p_re * re - p_im * im, p_re * im + p_im * re)

        by_rows(first)
        transform()

        def propagate(row):
            rows = pl.ds(row, ROWS)
            h_re, h_im = prop[0, rows, :], prop[1, rows, :]
            for s in range(slots):
                re, im = result(s, row)
                put(s, row, re * h_im + im * h_re, re * h_re - im * h_im)

        by_rows(propagate)
        forward(it, 2)
        transform()
        forward(it, 3)
        for k in (2, 3):
            landed(it, k)

        def second(row):
            rows = pl.ds(row, ROWS)
            for s in range(slots):
                m_im, m_re = result(s, row)
                re, im = window(it, s, row, 2), window(it, s, row, 3)
                mid_buf[s, 0, rows, :], mid_buf[s, 1, rows, :] = m_re, m_im
                win_buf[s, 0, rows, :], win_buf[s, 1, rows, :] = re, im
                put(s, row, m_re * re - m_im * im, m_re * im + m_im * re)

        by_rows(second)
        transform()

        def compare(row):
            rows = pl.ds(row, ROWS)
            for s in range(slots):
                re, im = result(s, row)
                factor = 1.0 - amps[it, 0, 0, s, rows, :] * lax.rsqrt(re * re + im * im + SOFT_FLOOR)
                put(s, row, im * factor, re * factor)

        by_rows(compare)
        transform()

        def back(row):
            rows = pl.ds(row, ROWS)
            found = [[], []]
            for s in range(slots):
                im, re = result(s, row)
                m_re, m_im = mid_buf[s, 0, rows, :], mid_buf[s, 1, rows, :]
                w_re, w_im = win_buf[s, 0, rows, :], win_buf[s, 1, rows, :]
                found[0].append(m_re * re + m_im * im)
                found[1].append(m_re * im - m_im * re)
                put(s, row, w_re * re + w_im * im, w_re * im - w_im * re)
            place(it, row, 2, found[0])
            place(it, row, 3, found[1])

        by_rows(back)
        give_right(it, 1)
        transform()

        def turn(row):
            rows = pl.ds(row, ROWS)
            h_re, h_im = prop[0, rows, :], prop[1, rows, :]
            for s in range(slots):
                re, im = result(s, row)
                put(s, row, im * h_re - re * h_im, re * h_re + im * h_im)

        by_rows(turn)
        give_down(it, 1)
        transform()

        def early(row):
            rows = pl.ds(row, ROWS)
            found = [[], []]
            for s in range(slots):
                im, re = result(s, row)
                p_re, p_im = rolled[it, s, 0, rows, :], rolled[it, s, 1, rows, :]
                found[0].append(p_re * re + p_im * im)
                found[1].append(p_re * im - p_im * re)
            place(it, row, 0, found[0])
            place(it, row, 1, found[1])

        by_rows(early)
        give_right(it, 0)
        give_down(it, 0)
        for k in (2, 3):
            update(it, k)
        for k in (0, 1):
            update(it, k)
            if it < iters - 1:
                send(it + 1, k)
        for k in (2, 3):
            if it < iters - 1:
                send(it + 1, k)

    for it in range(iters):
        for kind in range(6):
            for k in range(4):
                copy(it, kind, k).wait_send()


def shards(ny, nx, object_tiles, probe_field, prop_angle, scan_offsets, probe_counts, amplitudes):
    n = object_tiles.shape[2]
    iters, slots = scan_offsets.shape[0], scan_offsets.shape[3]
    left_table, right_table = dft_tables(n)
    vmem, smem = pl.BlockSpec(memory_space=pltpu.VMEM), pl.BlockSpec(memory_space=pltpu.SMEM)
    rolled, prop = pl.pallas_call(
        prepare_kernel,
        out_shape=[
            jax.ShapeDtypeStruct((iters, slots, 2, n, n), jnp.float32),
            jax.ShapeDtypeStruct((2, n, n), jnp.float32),
        ],
        in_specs=[smem, vmem, vmem],
        out_specs=[vmem, vmem],
        compiler_params=pltpu.CompilerParams(vmem_limit_bytes=32 * 2**20),
    )(scan_offsets, probe_field, prop_angle)
    f32, bf16 = jnp.float32, jnp.bfloat16
    return pl.pallas_call(
        functools.partial(kernel, ny, nx),
        out_shape=jax.ShapeDtypeStruct(object_tiles.shape, f32),
        in_specs=[smem, smem] + [pl.BlockSpec(memory_space=pltpu.HBM)] * 6,
        out_specs=vmem,
        scratch_shapes=[
            pltpu.VMEM(object_tiles.shape, f32),
            pltpu.VMEM(rolled.shape, f32),
            pltpu.VMEM(prop.shape, f32),
            pltpu.VMEM(amplitudes.shape, f32),
            pltpu.VMEM(left_table.shape, bf16),
            pltpu.VMEM(right_table.shape, bf16),
            pltpu.SemaphoreType.DMA((6,)),
            pltpu.VMEM(object_tiles.shape, f32),
            pltpu.VMEM((iters, 4, 4, n, n), f32),
            pltpu.VMEM((iters, 4, 4, n, n), f32),
            pltpu.VMEM((iters, 3, 4, n, n), f32),
            pltpu.VMEM((6 * n, slots * n), bf16),
            pltpu.VMEM((2 * n, slots * n), f32),
            pltpu.VMEM((slots * n, 6 * n), bf16),
            pltpu.VMEM((slots * n, 2 * n), f32),
            pltpu.VMEM((slots, 2, n, n), f32),
            pltpu.VMEM((slots, 2, n, n), f32),
            pltpu.SemaphoreType.DMA((iters, 6, 4)),
            pltpu.SemaphoreType.DMA((iters, 6, 4)),
        ],
        compiler_params=pltpu.CompilerParams(
            collective_id=0, has_side_effects=True, vmem_limit_bytes=56 * 2**20
        ),
    )(scan_offsets, probe_counts, object_tiles, rolled, prop, amplitudes,
      jnp.asarray(left_table), jnp.asarray(right_table))


def solution(mesh):
    in_specs = (
        P(None, None, "ty", "tx"),
        P(),
        P(),
        P(None, "ty", "tx", None, None),
        P(None, "ty", "tx"),
        P(None, "ty", "tx", None, None, None),
    )
    return jax.shard_map(
        functools.partial(shards, mesh.shape["ty"], mesh.shape["tx"]),
        mesh=mesh, in_specs=in_specs, out_specs=P(None, None, "ty", "tx"), check_vma=False,
    )
```
